32 devices in a mesh: row: 16 (over z, y, x), col: 2 (over core).
Axes of the slice: x: 2, y: 2, z: 4, core: 2. Of those that a mesh axis runs over, the one named last changes fastest.
Arguments:
- points: float32 [8, 8192], P(None, 'row'), may hold values from -6 to 6
- lengthscale: float32 [8], replicated, may hold values from 1 to 3
- noise: float32 [8192], P('row'), may hold values from 0.3 to 3
- target: float32 [8192], P('row'), may hold values from -6 to 6
- probe_bits: int32 [8, 8192], P(None, 'row'), may hold values from 0 to 1
Outputs:
- solution: float32 [9, 8192], P(None, 'row')
- residual: float32 [9, 8192], P(None, 'row')
The draws below stay inside these ranges and needn't reach their ends.
All inputs are finite; a program needn't handle non-finite values.
Results may differ from the reference program's by a relative error of at most 0.0003.
Values sent between devices are 32-bit elements; how exact they have to be, the bound alone decides.
A program may use at most 64 MiB of HBM per device.

```python
import math
import jax
import jax.numpy as jnp
from jax import lax

FEAT = 8
PROBES = 8
ITERS = 2
POINTS = 8192


def with_ends(values, own_key, least, largest):
    longest = values.shape.index(max(values.shape))
    spots = []
    for shift in (0, 1):
        where = [jax.random.randint(jax.random.fold_in(own_key, axis), (), 0, length) for axis, length in enumerate(values.shape)]
        where[longest] = (where[longest] + shift) % values.shape[longest]
        spots.append(tuple(where))
    return values.at[spots[0]].set(least).at[spots[1]].set(largest)


def steps_of(rng, shape, split, low, largest):
    level, own = 1.0, jax.random.fold_in(rng, 6)
    for position, blocks in split:
        steps = jnp.exp(jax.random.uniform(jax.random.fold_in(own, position), (blocks,), jnp.float32, low / len(split), largest / len(split)))
        level = level * jnp.repeat(steps, shape[position] // blocks).reshape([-1 if axis == position else 1 for axis in range(len(shape))])
    return level


def normal_values(key, shape, width, bound, split=(), kind=jnp.bfloat16):
    gain = steps_of(key, shape, split, -0.22, 0.18) if split else 1.0
    result = jax.random.normal(key, shape, jnp.float32) * width * gain
    return jnp.minimum(jnp.maximum(result, -bound), bound).astype(kind)


def setup_inputs(seed: int = 0) -> dict:
    streams_of = jax.random.split(jax.random.key(seed), 6)
    return {
        "points": normal_values(streams_of[0], (FEAT, POINTS), 1.0, 6.0, ((1, 16),), jnp.float32),
        "lengthscale": jnp.clip(jnp.exp(jax.random.uniform(streams_of[1], (FEAT,), jnp.float32, math.log(1.0), math.log(3.0))), 1.0, 3.0),
        "noise": jnp.clip(jnp.exp(math.log(3.0) - 2.3025851 * jax.random.uniform(streams_of[2], (POINTS,), jnp.float32) ** steps_of(streams_of[2], (POINTS,), ((0, 16),), -0.2, 0.2)), 0.3, 3.0),
        "target": normal_values(streams_of[3], (POINTS,), 1.0, 6.0, ((0, 16),), jnp.float32),
        "probe_bits": with_ends(jax.random.randint(streams_of[4], (PROBES, POINTS), 0, 2), jax.random.fold_in(streams_of[4], 1), 0, 1).astype(jnp.int32),
    }


root_five = 5.0 ** 0.5

def matern_values(dist_sq):
    scaled_dist = root_five * jnp.sqrt(dist_sq)
    return (1.0 + scaled_dist + scaled_dist * scaled_dist / 3.0) * jnp.exp(-scaled_dist)

def apply_kernel(scaled, direction):
    total = scaled.shape[1]
    block = min(512, total)
    count = total // block

    def one_block(index_block):
        rows_here = lax.dynamic_slice_in_dim(scaled, (index_block * block).astype(jnp.int32), block, 1)
        dist_sq = jnp.zeros((block, total), jnp.float32)
        for feature in range(scaled.shape[0]):
            offset = rows_here[feature][:, None] - scaled[feature][None, :]
            dist_sq = dist_sq + offset * offset
        kernel_rows = matern_values(dist_sq)
        return jnp.dot(kernel_rows, direction.T, precision=lax.Precision.HIGHEST, preferred_element_type=jnp.float32)
    pieces = lax.map(one_block, jnp.arange(count, dtype=jnp.int32))
    return pieces.reshape(total, direction.shape[0]).T

def reference(points, lengthscale, noise, target, probe_bits):
    scaled = points / lengthscale[:, None]
    signs = 2.0 * probe_bits.astype(jnp.float32) - 1.0
    rhs = jnp.concatenate([signs, target[None, :]], axis=0)
    solution = jnp.zeros_like(rhs)
    residual = rhs
    direction = rhs
    norm_now = lax.optimization_barrier(jnp.sum(residual * residual, axis=1))
    for iteration in range(ITERS):
        image = apply_kernel(scaled, direction) + noise[None, :] * direction
        alpha = norm_now / lax.optimization_barrier(jnp.sum(direction * image, axis=1))
        solution = solution + alpha[:, None] * direction
        residual = residual - alpha[:, None] * image
        if iteration + 1 < ITERS:
            norm_next = lax.optimization_barrier(jnp.sum(residual * residual, axis=1))
            direction = residual + (norm_next / norm_now)[:, None] * direction
            norm_now = norm_next
    return (solution, residual)
```

```python
import functools

import jax
import jax.numpy as jnp
from jax import lax
from jax.experimental import pallas as pl
from jax.experimental.pallas import tpu as pltpu
from jax.sharding import PartitionSpec as P

MESH = pl.DeviceIdType.MESH
LANES = 128
root_five = 5.0**0.5


def split(x):
    high = x.astype(jnp.bfloat16).astype(jnp.float32)
    rest = x - high
    mid = rest.astype(jnp.bfloat16).astype(jnp.float32)
    return high, mid, rest - mid


def augment(points, own):
    high, mid, low = split(points)
    norms = split(jnp.sum(points * points, axis=0, keepdims=True))
    rows = lax.broadcasted_iota(jnp.int32, points.shape, 0)
    first = 3 if own else 0
    ends = jnp.where(rows < 6, 1.0, 0.0)
    for place in range(3):
        ends = jnp.where(rows == first + place, norms[place], ends)
    if own:
        high, mid, low = -2.0 * high, -2.0 * mid, -2.0 * low
        parts = [high, mid, high, low, high, mid]
    else:
        parts = [high, high, mid, high, low, mid]
    return jnp.concatenate(parts + [ends, jnp.zeros_like(ends)], axis=0)


def sixteen(probes, tile):
    n = probes.shape[1]
    line = jnp.concatenate([tile[k : k + 1, :] for k in range(n // LANES)], axis=1)
    rows = lax.broadcasted_iota(jnp.int32, probes.shape, 0)
    return jnp.concatenate([probes, jnp.where(rows == 0, line, 0.0)], axis=0)


def halves(x):
    high = x.astype(jnp.bfloat16)
    mid = (x - high.astype(jnp.float32)).astype(jnp.bfloat16)
    return jnp.concatenate([high, mid], axis=0)


def scalars(values):
    lanes = lax.broadcasted_iota(jnp.int32, (8, LANES), 1)
    tile = jnp.zeros((8, LANES), jnp.float32)
    for k, value in enumerate(values):
        tile = jnp.where(lanes == k, value[0:8], tile)
        tile = jnp.where(lanes == len(values) + k, value[8:9], tile)
    return tile


def kernel(R, C, scale, points, noise, target, bits, sol, res,
           msg, slots_a, parts, vec, slots_b, scal_b, own_c, scal_c, k_hi, k_lo,
           send_a, recv_a, send_p, recv_p, send_b, recv_b, send_s, recv_s, send_c, recv_c):
    n = points.shape[1]
    G = R // C
    T = R // C
    sub = min(256, n)
    me_r = lax.axis_index("row")
    me_c = lax.axis_index("col")
    group = me_r // G
    spot = lax.rem(me_r, G)
    side = lax.rem(me_r, C)
    in_group = group == me_c

    barrier = pltpu.get_barrier_semaphore()

    def greet(k, carry):
        pl.semaphore_signal(barrier, inc=1, device_id=(lax.rem(me_r + k, R), side), device_id_type=MESH)
        return carry

    lax.fori_loop(1, R, greet, 0)
    for k in range(1, C):
        pl.semaphore_signal(barrier, inc=1, device_id=(me_r, lax.rem(me_c + k, C)), device_id_type=MESH)

    rows8 = lax.broadcasted_iota(jnp.int32, (8, 1), 0)
    lengths = jnp.full((8, 1), scale[0], jnp.float32)
    for f in range(1, 8):
        lengths = jnp.where(rows8 == f, scale[f], lengths)
    own_points = points[...] * (root_five / lengths)
    signs = 2.0 * bits[...].astype(jnp.float32) - 1.0
    own_target = target[...]
    msg[:, 0:n] = own_points
    msg[:, n : 2 * n] = signs
    msg[:, 2 * n :] = jnp.zeros((8, LANES), jnp.float32)
    for k in range(n // LANES):
        msg[k : k + 1, 2 * n :] = own_target[:, k * LANES : (k + 1) * LANES]

    pl.semaphore_wait(barrier, (T - jnp.where(side == me_c, 1, 0)) * C + C - 1)

    def target_row(k):
        return C * lax.rem(me_r // C + k, T) + me_c

    def copy_a(k):
        return pltpu.make_async_remote_copy(
            src_ref=msg, dst_ref=slots_a.at[spot], send_sem=send_a.at[k], recv_sem=recv_a.at[spot],
            device_id=(target_row(k), group), device_id_type=MESH)

    def copy_p(phase, k):
        return pltpu.make_async_remote_copy(
            src_ref=parts.at[phase, me_c], dst_ref=parts.at[phase, me_c],
            send_sem=send_p.at[phase, k - 1], recv_sem=recv_p.at[phase, me_c],
            device_id=(me_r, lax.rem(me_c + k, C)), device_id_type=MESH)

    def copy_b(k):
        return pltpu.make_async_remote_copy(
            src_ref=vec, dst_ref=slots_b.at[spot], send_sem=send_b.at[k], recv_sem=recv_b.at[spot],
            device_id=(target_row(k), group), device_id_type=MESH)

    def copy_s(k, g):
        return pltpu.make_async_remote_copy(
            src_ref=scal_b.at[me_r], dst_ref=scal_b.at[me_r], send_sem=send_s.at[g - 1, k], recv_sem=recv_s.at[me_r],
            device_id=(target_row(k), lax.rem(group + g, C)), device_id_type=MESH)

    def copy_c(k, g):
        return pltpu.make_async_remote_copy(
            src_ref=own_c, dst_ref=scal_c.at[me_r], send_sem=send_c.at[g, k], recv_sem=recv_c.at[me_r],
            device_id=(target_row(k), g), device_id_type=MESH)

    def over_targets(action):
        def one(k, carry):
            @pl.when(target_row(k) != me_r)
            def _():
                action(k)
            return carry
        lax.fori_loop(0, T, one, 0)

    over_targets(lambda k: copy_a(k).start())

    @pl.when(in_group)
    def _():
        slots_a[spot] = msg[...]

    own_aug = augment(own_points, True).astype(jnp.bfloat16)

    def wait_slot(buffer, sem, t, like):
        pltpu.make_async_remote_copy(
            src_ref=like, dst_ref=buffer.at[t], send_sem=send_a.at[0], recv_sem=sem.at[t],
            device_id=(me_r, me_c), device_id_type=MESH).wait_recv()

    def build(k, accum):
        t = lax.rem(spot + k, G)

        @pl.when(me_c * G + t != me_r)
        def _():
            wait_slot(slots_a, recv_a, t, msg)

        columns = augment(slots_a[t, :, 0:n], False).T.astype(jnp.bfloat16)
        dirs = halves(sixteen(slots_a[t, :, n : 2 * n], slots_a[t, :, 2 * n :]))
        for j in range(0, n, sub):
            s2 = jnp.dot(columns[j : j + sub, :], own_aug, preferred_element_type=jnp.float32)
            s2 = jnp.maximum(s2, 1e-12)
            s = s2 * lax.rsqrt(s2)
            value = (s2 * (1.0 / 3.0) + s + 1.0) * jnp.exp(-s)
            high = value.astype(jnp.bfloat16)
            low = (value - high.astype(jnp.float32)).astype(jnp.bfloat16)
            k_hi[t, j : j + sub, :] = high
            k_lo[t, j : j + sub, :] = low
            here = dirs[:, j : j + sub]
            accum = accum + jnp.dot(here, high, preferred_element_type=jnp.float32)
            accum = accum + jnp.dot(here, low, preferred_element_type=jnp.float32)
        return accum

    zero = jnp.zeros((32, n), jnp.float32)
    accum = lax.fori_loop(0, G, build, zero)

    def across(phase, accum):
        parts[phase, me_c] = accum[0:16] + accum[16:32]
        for k in range(1, C):
            copy_p(phase, k).start()
        for k in range(1, C):
            c = lax.rem(me_c + k, C)
            pltpu.make_async_remote_copy(
                src_ref=parts.at[phase, me_c], dst_ref=parts.at[phase, c], send_sem=send_p.at[phase, 0],
                recv_sem=recv_p.at[phase, c], device_id=(me_r, me_c), device_id_type=MESH).wait_recv()
        total = parts[phase, 0]
        for c in range(1, C):
            total = total + parts[phase, c]
        return total

    noise_row = noise[...]
    start = sixteen(signs, msg[:, 2 * n :])
    image = across(0, accum) + noise_row * start

    def dot(a, b):
        return jnp.sum(a * b, axis=1, keepdims=True)

    own_scal = scalars([dot(start, image), dot(image, image), dot(start, start)])
    vec[:, 0:n] = image[0:8]
    vec[:, n : n + LANES] = jnp.zeros((8, LANES), jnp.float32)
    for k in range(n // LANES):
        vec[k : k + 1, n : n + LANES] = image[8:9, k * LANES : (k + 1) * LANES]
    vec[:, n + LANES :] = own_scal
    scal_b[me_r] = own_scal

    def send_image(k):
        copy_b(k).start()
        for g in range(1, C):
            copy_s(k, g).start()

    over_targets(send_image)

    @pl.when(in_group)
    def _():
        slots_b[spot] = vec[...]

    def receive_image(b, carry):
        @pl.when(b != me_r)
        def _():
            @pl.when(b // G == me_c)
            def _():
                t = lax.rem(b, G)
                wait_slot(slots_b, recv_b, t, vec)
                scal_b[b] = slots_b[t, :, n + LANES :]

            @pl.when(b // G != me_c)
            def _():
                wait_slot(scal_b, recv_s, b, own_c)
        return carry

    lax.fori_loop(0, R, receive_image, 0)
    total = jnp.sum(scal_b[...], axis=0)

    def pick(tile, k, count):
        return jnp.concatenate([tile[:, k : k + 1], tile[:, count + k : count + k + 1]], axis=0)

    curve, square, norm = pick(total, 0, 3), pick(total, 1, 3), pick(total, 2, 3)
    alpha = norm / curve
    norm_next = alpha * alpha * square - norm
    beta = norm_next / norm

    def again(t, accum):
        first = sixteen(slots_a[t, :, n : 2 * n], slots_a[t, :, 2 * n :])
        moved = sixteen(slots_b[t, :, 0:n], slots_b[t, :, n : n + LANES])
        dirs = halves((first - alpha * moved) + beta * first)
        accum = accum + jnp.dot(dirs, k_hi[t], preferred_element_type=jnp.float32)
        return accum + jnp.dot(dirs, k_lo[t], preferred_element_type=jnp.float32)

    accum = lax.fori_loop(0, G, again, zero)
    residual = start - alpha * image
    direction = residual + beta * start
    image = across(1, accum) + noise_row * direction
    own_scal = scalars([dot(direction, image)])
    own_c[...] = own_scal
    scal_c[me_r] = own_scal

    def send_curve(k):
        for g in range(C):
            copy_c(k, g).start()

    over_targets(send_curve)

    def receive_curve(b, carry):
        @pl.when(b != me_r)
        def _():
            wait_slot(scal_c, recv_c, b, own_c)
        return carry

    lax.fori_loop(0, R, receive_curve, 0)
    alpha_last = norm_next / pick(jnp.sum(scal_c[...], axis=0), 0, 1)
    answer = alpha * start + alpha_last * direction
    residual = residual - alpha_last * image
    sol[0:8, :] = answer[0:8]
    sol[8:9, :] = answer[8:9]
    res[0:8, :] = residual[0:8]
    res[8:9, :] = residual[8:9]

    def finish(k):
        copy_a(k).wait_send()
        copy_b(k).wait_send()
        for g in range(1, C):
            copy_s(k, g).wait_send()
        for g in range(C):
            copy_c(k, g).wait_send()

    over_targets(finish)
    for phase in range(2):
        for k in range(1, C):
            copy_p(phase, k).wait_send()


def per_device(R, C, points, lengthscale, noise, target, probe_bits):
    n = points.shape[1]
    G = T = R // C
    f32, bf16, dma = jnp.float32, jnp.bfloat16, pltpu.SemaphoreType.DMA
    vmem = pl.BlockSpec(memory_space=pltpu.VMEM)
    return pl.pallas_call(
        functools.partial(kernel, R, C),
        out_shape=(jax.ShapeDtypeStruct((9, n), f32),) * 2,
        in_specs=[pl.BlockSpec(memory_space=pltpu.SMEM)] + [vmem] * 4,
        out_specs=(vmem, vmem),
        scratch_shapes=[
            pltpu.VMEM((8, 2 * n + LANES), f32),
            pltpu.VMEM((G, 8, 2 * n + LANES), f32),
            pltpu.VMEM((2, C, 16, n), f32),
            pltpu.VMEM((8, n + 2 * LANES), f32),
            pltpu.VMEM((G, 8, n + 2 * LANES), f32),
            pltpu.VMEM((R, 8, LANES), f32),
            pltpu.VMEM((8, LANES), f32),
            pltpu.VMEM((R, 8, LANES), f32),
            pltpu.VMEM((G, n, n), bf16),
            pltpu.VMEM((G, n, n), bf16),
            dma((T,)), dma((G,)), dma((2, C - 1)), dma((2, C)), dma((T,)), dma((G,)),
            dma((C - 1, T)), dma((R,)), dma((C, T)), dma((R,)),
        ],
        compiler_params=pltpu.CompilerParams(
            collective_id=0, has_side_effects=True, vmem_limit_bytes=40 * 1024 * 1024
        ),
    )(lengthscale, points, noise.reshape(1, n), target.reshape(1, n), probe_bits)


def solution(mesh):
    return jax.shard_map(
        functools.partial(per_device, mesh.shape["row"], mesh.shape["col"]),
        mesh=mesh,
        in_specs=(P(None, "row"), P(), P("row"), P("row"), P(None, "row")),
        out_specs=(P(None, "row"), P(None, "row")),
        check_vma=False,
    )
```

```python
import functools

import jax
import jax.numpy as jnp
from jax import lax
from jax.experimental import pallas as pl
from jax.experimental.pallas import tpu as pltpu
from jax.sharding import PartitionSpec as P

MESH = pl.DeviceIdType.MESH
LANES = 128
root_five = 5.0**0.5


def split(x):
    high = x.astype(jnp.bfloat16).astype(jnp.float32)
    rest = x - high
    mid = rest.astype(jnp.bfloat16).astype(jnp.float32)
    return high, mid, rest - mid


def augment(points, own):
    high, mid, low = split(points)
    norms = split(jnp.sum(points * points, axis=0, keepdims=True))
    rows = lax.broadcasted_iota(jnp.int32, points.shape, 0)
    first = 3 if own else 0
    ends = jnp.where(rows < 6, 1.0, 0.0)
    for place in range(3):
        ends = jnp.where(rows == first + place, norms[place], ends)
    if own:
        high, mid, low = -2.0 * high, -2.0 * mid, -2.0 * low
        parts = [high, mid, high, low, high, mid]
    else:
        parts = [high, high, mid, high, low, mid]
    return jnp.concatenate(parts + [ends, jnp.zeros_like(ends)], axis=0)


def sixteen(probes, tile):
    n = probes.shape[1]
    line = jnp.concatenate([tile[k : k + 1, :] for k in range(n // LANES)], axis=1)
    rows = lax.broadcasted_iota(jnp.int32, probes.shape, 0)
    return jnp.concatenate([probes, jnp.where(rows == 0, line, 0.0)], axis=0)


def halves(x):
    high = x.astype(jnp.bfloat16)
    mid = (x - high.astype(jnp.float32)).astype(jnp.bfloat16)
    return jnp.concatenate([high, mid], axis=0)


def scalars(values):
    lanes = lax.broadcasted_iota(jnp.int32, (8, LANES), 1)
    tile = jnp.zeros((8, LANES), jnp.float32)
    for k, value in enumerate(values):
        tile = jnp.where(lanes == k, value[0:8], tile)
        tile = jnp.where(lanes == len(values) + k, value[8:9], tile)
    return tile


def kernel(R, C, scale_in, points_in, noise_in, target_in, bits_in, sol, res,
           scale, points, noise, target, bits, msg, slots_a, msg_v, slots_v, parts, vec, slots_b, scal_b, own_c, scal_c, k_hi, k_lo,
           load, send_a, recv_a, send_v, recv_v, send_p, recv_p, send_b, recv_b, send_s, recv_s, send_c, recv_c):
    n = points.shape[1]
    G = R // C
    T = R // C
    sub = min(256, n)
    me_r = lax.axis_index("row")
    me_c = lax.axis_index("col")
    group = me_r // G
    spot = lax.rem(me_r, G)
    side = lax.rem(me_r, C)
    in_group = group == me_c

    loads = [
        pltpu.make_async_copy(source, here, load.at[k])
        for k, (source, here) in enumerate(
            [(scale_in, scale), (points_in, points), (bits_in, bits), (target_in, target), (noise_in, noise)])
    ]
    for one in loads:
        one.start()

    barrier = pltpu.get_barrier_semaphore()

    def greet(k, carry):
        pl.semaphore_signal(barrier, inc=1, device_id=(lax.rem(me_r + k, R), side), device_id_type=MESH)
        return carry

    lax.fori_loop(1, R, greet, 0)
    for k in range(1, C):
        pl.semaphore_signal(barrier, inc=1, device_id=(me_r, lax.rem(me_c + k, C)), device_id_type=MESH)

    for one in loads:
        one.wait()

    rows8 = lax.broadcasted_iota(jnp.int32, (8, 1), 0)
    lengths = jnp.full((8, 1), scale[0], jnp.float32)
    for f in range(1, 8):
        lengths = jnp.where(rows8 == f, scale[f], lengths)
    own_points = points[...] * (root_five / lengths)
    signs = 2.0 * bits[...].astype(jnp.float32) - 1.0
    own_target = target[...]
    msg[...] = own_points
    msg_v[:, 0:n] = signs
    msg_v[:, n:] = jnp.zeros((8, LANES), jnp.float32)
    for k in range(n // LANES):
        msg_v[k : k + 1, n:] = own_target[:, k * LANES : (k + 1) * LANES]

    pl.semaphore_wait(barrier, (T - jnp.where(side == me_c, 1, 0)) * C + C - 1)

    def target_row(k):
        return C * lax.rem(me_r // C + k, T) + me_c

    def copy_a(k):
        return pltpu.make_async_remote_copy(
            src_ref=msg, dst_ref=slots_a.at[spot], send_sem=send_a.at[k], recv_sem=recv_a.at[spot],
            device_id=(target_row(k), group), device_id_type=MESH)

    def copy_v(k):
        return pltpu.make_async_remote_copy(
            src_ref=msg_v, dst_ref=slots_v.at[spot], send_sem=send_v.at[k], recv_sem=recv_v.at[spot],
            device_id=(target_row(k), group), device_id_type=MESH)

    def copy_p(phase, k):
        return pltpu.make_async_remote_copy(
            src_ref=parts.at[phase, me_c], dst_ref=parts.at[phase, me_c],
            send_sem=send_p.at[phase, k - 1], recv_sem=recv_p.at[phase, me_c],
            device_id=(me_r, lax.rem(me_c + k, C)), device_id_type=MESH)

    def copy_b(k):
        return pltpu.make_async_remote_copy(
            src_ref=vec, dst_ref=slots_b.at[spot], send_sem=send_b.at[k], recv_sem=recv_b.at[spot],
            device_id=(target_row(k), group), device_id_type=MESH)

    def copy_s(k, g):
        return pltpu.make_async_remote_copy(
            src_ref=scal_b.at[me_r], dst_ref=scal_b.at[me_r], send_sem=send_s.at[g - 1, k], recv_sem=recv_s.at[me_r],
            device_id=(target_row(k), lax.rem(group + g, C)), device_id_type=MESH)

    def copy_c(k, g):
        return pltpu.make_async_remote_copy(
            src_ref=own_c, dst_ref=scal_c.at[me_r], send_sem=send_c.at[g, k], recv_sem=recv_c.at[me_r],
            device_id=(target_row(k), g), device_id_type=MESH)

    def over_targets(action):
        def one(k, carry):
            @pl.when(target_row(k) != me_r)
            def _():
                action(k)
            return carry
        lax.fori_loop(0, T, one, 0)

    over_targets(lambda k: (copy_a(k).start(), copy_v(k).start()))

    @pl.when(in_group)
    def _():
        slots_a[spot] = msg[...]
        slots_v[spot] = msg_v[...]

    own_aug = augment(own_points, True).astype(jnp.bfloat16)

    def wait_slot(buffer, sem, t, like):
        pltpu.make_async_remote_copy(
            src_ref=like, dst_ref=buffer.at[t], send_sem=send_a.at[0], recv_sem=sem.at[t],
            device_id=(me_r, me_c), device_id_type=MESH).wait_recv()

    first_spot = jnp.where(in_group, spot, G - 1)

    def at(k):
        return lax.rem(first_spot - k + G, G)

    def arrive(buffer, sem, t, like):
        @pl.when(me_c * G + t != me_r)
        def _():
            wait_slot(buffer, sem, t, like)

    def build(t):
        columns = augment(slots_a[t], False).T.astype(jnp.bfloat16)
        for j in range(0, n, sub):
            s2 = jnp.dot(columns[j : j + sub, :], own_aug, preferred_element_type=jnp.float32)
            s2 = jnp.maximum(s2, 1e-12)
            s = s2 * lax.rsqrt(s2)
            value = (s2 * (1.0 / 3.0) + s + 1.0) * jnp.exp(-s)
            top = value.astype(jnp.bfloat16)
            k_hi[t, j : j + sub, :] = top
            k_lo[t, j : j + sub, :] = (value - top.astype(jnp.float32)).astype(jnp.bfloat16)

    def multiply(t, dirs, accum):
        accum = accum + jnp.dot(dirs, k_hi[t], preferred_element_type=jnp.float32)
        return accum + jnp.dot(dirs, k_lo[t], preferred_element_type=jnp.float32)

    def first_of(t):
        return sixteen(slots_v[t, :, 0:n], slots_v[t, :, n:])

    def step(k, accum):
        arrive(slots_a, recv_a, at(k), msg)
        arrive(slots_v, recv_v, at(k - 1), msg_v)
        accum = multiply(at(k - 1), halves(first_of(at(k - 1))), accum)
        build(at(k))
        return accum

    zero = jnp.zeros((32, n), jnp.float32)
    arrive(slots_a, recv_a, at(0), msg)
    build(at(0))
    accum = lax.fori_loop(1, G, step, zero)
    arrive(slots_v, recv_v, at(G - 1), msg_v)
    accum = multiply(at(G - 1), halves(first_of(at(G - 1))), accum)

    def across(phase, accum):
        parts[phase, me_c] = accum[0:16] + accum[16:32]
        for k in range(1, C):
            copy_p(phase, k).start()
        for k in range(1, C):
            c = lax.rem(me_c + k, C)
            pltpu.make_async_remote_copy(
                src_ref=parts.at[phase, me_c], dst_ref=parts.at[phase, c], send_sem=send_p.at[phase, 0],
                recv_sem=recv_p.at[phase, c], device_id=(me_r, me_c), device_id_type=MESH).wait_recv()
        total = parts[phase, 0]
        for c in range(1, C):
            total = total + parts[phase, c]
        return total

    noise_row = noise[...]
    start = sixteen(signs, msg_v[:, n:])
    image = across(0, accum) + noise_row * start

    def dot(a, b):
        return jnp.sum(a * b, axis=1, keepdims=True)

    own_scal = scalars([dot(start, image), dot(image, image), dot(start, start)])
    vec[:, 0:n] = image[0:8]
    vec[:, n : n + LANES] = jnp.zeros((8, LANES), jnp.float32)
    for k in range(n // LANES):
        vec[k : k + 1, n : n + LANES] = image[8:9, k * LANES : (k + 1) * LANES]
    vec[:, n + LANES :] = own_scal
    scal_b[me_r] = own_scal

    def send_image(k):
        copy_b(k).start()
        for g in range(1, C):
            copy_s(k, g).start()

    over_targets(send_image)

    @pl.when(in_group)
    def _():
        slots_b[spot] = vec[...]

    def receive_image(b, carry):
        @pl.when(b != me_r)
        def _():
            @pl.when(b // G == me_c)
            def _():
                t = lax.rem(b, G)
                wait_slot(slots_b, recv_b, t, vec)
                scal_b[b] = slots_b[t, :, n + LANES :]

            @pl.when(b // G != me_c)
            def _():
                wait_slot(scal_b, recv_s, b, own_c)
        return carry

    lax.fori_loop(0, R, receive_image, 0)
    total = jnp.sum(scal_b[...], axis=0)

    def pick(tile, k, count):
        return jnp.concatenate([tile[:, k : k + 1], tile[:, count + k : count + k + 1]], axis=0)

    curve, square, norm = pick(total, 0, 3), pick(total, 1, 3), pick(total, 2, 3)
    alpha = norm / curve
    norm_next = alpha * alpha * square - norm
    beta = norm_next / norm

    def again(t, accum):
        first = first_of(t)
        moved = sixteen(slots_b[t, :, 0:n], slots_b[t, :, n : n + LANES])
        return multiply(t, halves((first - alpha * moved) + beta * first), accum)

    accum = lax.fori_loop(0, G, again, zero)
    residual = start - alpha * image
    direction = residual + beta * start
    image = across(1, accum) + noise_row * direction
    own_scal = scalars([dot(direction, image)])
    own_c[...] = own_scal
    scal_c[me_r] = own_scal

    def send_curve(k):
        for g in range(C):
            copy_c(k, g).start()

    over_targets(send_curve)

    def receive_curve(b, carry):
        @pl.when(b != me_r)
        def _():
            wait_slot(scal_c, recv_c, b, own_c)
        return carry

    lax.fori_loop(0, R, receive_curve, 0)
    alpha_last = norm_next / pick(jnp.sum(scal_c[...], axis=0), 0, 1)
    answer = alpha * start + alpha_last * direction
    residual = residual - alpha_last * image
    sol[0:8, :] = answer[0:8]
    sol[8:9, :] = answer[8:9]
    res[0:8, :] = residual[0:8]
    res[8:9, :] = residual[8:9]

    def finish(k):
        copy_a(k).wait_send()
        copy_v(k).wait_send()
        copy_b(k).wait_send()
        for g in range(1, C):
            copy_s(k, g).wait_send()
        for g in range(C):
            copy_c(k, g).wait_send()

    over_targets(finish)
    for phase in range(2):
        for k in range(1, C):
            copy_p(phase, k).wait_send()


def per_device(R, C, points, lengthscale, noise, target, probe_bits):
    n = points.shape[1]
    G = T = R // C
    f32, bf16, dma = jnp.float32, jnp.bfloat16, pltpu.SemaphoreType.DMA
    vmem = pl.BlockSpec(memory_space=pltpu.VMEM)
    return pl.pallas_call(
        functools.partial(kernel, R, C),
        out_shape=(jax.ShapeDtypeStruct((9, n), f32),) * 2,
        in_specs=[pl.BlockSpec(memory_space=pl.ANY)] * 5,
        out_specs=(vmem, vmem),
        scratch_shapes=[
            pltpu.SMEM((8,), f32),
            pltpu.VMEM((8, n), f32),
            pltpu.VMEM((1, n), f32),
            pltpu.VMEM((1, n), f32),
            pltpu.VMEM((8, n), jnp.int32),
            pltpu.VMEM((8, n), f32),
            pltpu.VMEM((G, 8, n), f32),
            pltpu.VMEM((8, n + LANES), f32),
            pltpu.VMEM((G, 8, n + LANES), f32),
            pltpu.VMEM((2, C, 16, n), f32),
            pltpu.VMEM((8, n + 2 * LANES), f32),
            pltpu.VMEM((G, 8, n + 2 * LANES), f32),
            pltpu.VMEM((R, 8, LANES), f32),
            pltpu.VMEM((8, LANES), f32),
            pltpu.VMEM((R, 8, LANES), f32),
            pltpu.VMEM((G, n, n), bf16),
            pltpu.VMEM((G, n, n), bf16),
            dma((5,)), dma((T,)), dma((G,)), dma((T,)), dma((G,)), dma((2, C - 1)), dma((2, C)), dma((T,)), dma((G,)),
            dma((C - 1, T)), dma((R,)), dma((C, T)), dma((R,)),
        ],
        compiler_params=pltpu.CompilerParams(
            collective_id=0, has_side_effects=True, vmem_limit_bytes=60 * 1024 * 1024
        ),
    )(lengthscale, points, noise.reshape(1, n), target.reshape(1, n), probe_bits)


def solution(mesh):
    return jax.shard_map(
        functools.partial(per_device, mesh.shape["row"], mesh.shape["col"]),
        mesh=mesh,
        in_specs=(P(None, "row"), P(), P("row"), P("row"), P(None, "row")),
        out_specs=(P(None, "row"), P(None, "row")),
        check_vma=False,
    )
```

```python
import functools

import jax
import jax.numpy as jnp
from jax import lax
from jax.experimental import pallas as pl
from jax.experimental.pallas import tpu as pltpu
from jax.sharding import PartitionSpec as P

MESH = pl.DeviceIdType.MESH
LANES = 128
root_five = 5.0**0.5


def split(x):
    high = x.astype(jnp.bfloat16).astype(jnp.float32)
    rest = x - high
    mid = rest.astype(jnp.bfloat16).astype(jnp.float32)
    return high, mid, rest - mid


def augment(points, own):
    high, mid, low = split(points)
    norms = split(jnp.sum(points * points, axis=0, keepdims=True))
    rows = lax.broadcasted_iota(jnp.int32, points.shape, 0)
    first = 3 if own else 0
    ends = jnp.where(rows < 6, 1.0, 0.0)
    for place in range(3):
        ends = jnp.where(rows == first + place, norms[place], ends)
    if own:
        high, mid, low = -2.0 * high, -2.0 * mid, -2.0 * low
        parts = [high, mid, high, low, high, mid]
    else:
        parts = [high, high, mid, high, low, mid]
    return jnp.concatenate(parts + [ends, jnp.zeros_like(ends)], axis=0)


def sixteen(probes, tile):
    n = probes.shape[1]
    line = jnp.concatenate([tile[k : k + 1, :] for k in range(n // LANES)], axis=1)
    rows = lax.broadcasted_iota(jnp.int32, probes.shape, 0)
    return jnp.concatenate([probes, jnp.where(rows == 0, line, 0.0)], axis=0)


def halves(x):
    high = x.astype(jnp.bfloat16)
    mid = (x - high.astype(jnp.float32)).astype(jnp.bfloat16)
    return jnp.concatenate([high, mid], axis=0)


def scalars(values):
    lanes = lax.broadcasted_iota(jnp.int32, (16, LANES), 1)
    rows = lax.broadcasted_iota(jnp.int32, (16, LANES), 0)
    spread = jnp.zeros((16, LANES), jnp.float32)
    for k, value in enumerate(values):
        spread = jnp.where(lanes == rows + 16 * k, value, spread)
    return jnp.sum(spread, axis=0, keepdims=True)


def pick(line, k):
    lanes = lax.broadcasted_iota(jnp.int32, (16, LANES), 1)
    rows = lax.broadcasted_iota(jnp.int32, (16, LANES), 0)
    return jnp.sum(jnp.where(lanes == rows + 16 * k, line, 0.0), axis=1, keepdims=True)


def kernel(R, C, scale_in, points_in, noise_in, target_in, bits_in, both,
           scale, points, noise, target, bits, msg, slots_a, msg_v, slots_v, parts, vec, slots_b, scal_b, own_c, scal_c, k_hi, k_lo,
           load, send_a, recv_a, send_v, recv_v, send_p, recv_p, send_b, recv_b, send_s, recv_s, send_c, recv_c):
    n = points.shape[1]
    G = R // C
    T = R // C
    sub = min(256, n)
    me_r = lax.axis_index("row")
    me_c = lax.axis_index("col")
    group = me_r // G
    spot = lax.rem(me_r, G)
    side = lax.rem(me_r, C)
    in_group = group == me_c

    loads = [
        pltpu.make_async_copy(source, here, load.at[k])
        for k, (source, here) in enumerate(
            [(scale_in, scale), (points_in, points), (bits_in, bits), (target_in, target), (noise_in, noise)])
    ]
    for one in loads:
        one.start()

    barrier = pltpu.get_barrier_semaphore()

    def greet(k, carry):
        pl.semaphore_signal(barrier, inc=1, device_id=(lax.rem(me_r + k, R), side), device_id_type=MESH)
        return carry

    lax.fori_loop(1, R, greet, 0)
    for k in range(1, C):
        pl.semaphore_signal(barrier, inc=1, device_id=(me_r, lax.rem(me_c + k, C)), device_id_type=MESH)

    for one in loads:
        one.wait()

    rows8 = lax.broadcasted_iota(jnp.int32, (8, 1), 0)
    lengths = jnp.full((8, 1), scale[0], jnp.float32)
    for f in range(1, 8):
        lengths = jnp.where(rows8 == f, scale[f], lengths)
    own_points = points[...] * (root_five / lengths)
    signs = 2.0 * bits[...].astype(jnp.float32) - 1.0
    own_target = target[...]
    msg[...] = own_points
    msg_v[:, 0:n] = signs
    msg_v[:, n:] = jnp.zeros((8, LANES), jnp.float32)
    for k in range(n // LANES):
        msg_v[k : k + 1, n:] = own_target[:, k * LANES : (k + 1) * LANES]

    pl.semaphore_wait(barrier, (T - jnp.where(side == me_c, 1, 0)) * C + C - 1)

    def target_row(k):
        return C * lax.rem(me_r // C + k, T) + me_c

    def copy_a(k):
        return pltpu.make_async_remote_copy(
            src_ref=msg, dst_ref=slots_a.at[spot], send_sem=send_a.at[k], recv_sem=recv_a.at[spot],
            device_id=(target_row(k), group), device_id_type=MESH)

    def copy_v(k):
        return pltpu.make_async_remote_copy(
            src_ref=msg_v, dst_ref=slots_v.at[spot], send_sem=send_v.at[k], recv_sem=recv_v.at[spot],
            device_id=(target_row(k), group), device_id_type=MESH)

    def copy_p(phase, k):
        return pltpu.make_async_remote_copy(
            src_ref=parts.at[phase, me_c], dst_ref=parts.at[phase, me_c],
            send_sem=send_p.at[phase, k - 1], recv_sem=recv_p.at[phase, me_c],
            device_id=(me_r, lax.rem(me_c + k, C)), device_id_type=MESH)

    def copy_b(k):
        return pltpu.make_async_remote_copy(
            src_ref=vec, dst_ref=slots_b.at[spot], send_sem=send_b.at[k], recv_sem=recv_b.at[spot],
            device_id=(target_row(k), group), device_id_type=MESH)

    def copy_s(k, g):
        return pltpu.make_async_remote_copy(
            src_ref=scal_b.at[me_r], dst_ref=scal_b.at[me_r], send_sem=send_s.at[g - 1, k], recv_sem=recv_s.at[me_r],
            device_id=(target_row(k), lax.rem(group + g, C)), device_id_type=MESH)

    def copy_c(k, g):
        return pltpu.make_async_remote_copy(
            src_ref=own_c, dst_ref=scal_c.at[me_r], send_sem=send_c.at[g, k], recv_sem=recv_c.at[me_r],
            device_id=(target_row(k), g), device_id_type=MESH)

    def over_targets(action):
        def one(k, carry):
            @pl.when(target_row(k) != me_r)
            def _():
                action(k)
            return carry
        lax.fori_loop(0, T, one, 0)

    over_targets(lambda k: (copy_a(k).start(), copy_v(k).start()))

    @pl.when(in_group)
    def _():
        slots_a[spot] = msg[...]
        slots_v[spot] = msg_v[...]

    own_aug = augment(own_points, True).astype(jnp.bfloat16)

    def wait_slot(buffer, sem, t, like):
        pltpu.make_async_remote_copy(
            src_ref=like, dst_ref=buffer.at[t], send_sem=send_a.at[0], recv_sem=sem.at[t],
            device_id=(me_r, me_c), device_id_type=MESH).wait_recv()

    first_spot = jnp.where(in_group, spot, G - 1)

    def at(k):
        return lax.rem(first_spot - k + G, G)

    def arrive(buffer, sem, t, like):
        @pl.when(me_c * G + t != me_r)
        def _():
            wait_slot(buffer, sem, t, like)

    def build(t):
        columns = augment(slots_a[t], False).T.astype(jnp.bfloat16)
        for j in range(0, n, sub):
            s2 = jnp.dot(columns[j : j + sub, :], own_aug, preferred_element_type=jnp.float32)
            s2 = jnp.maximum(s2, 1e-12)
            s = s2 * lax.rsqrt(s2)
            value = (s2 * (1.0 / 3.0) + s + 1.0) * jnp.exp(-s)
            top = value.astype(jnp.bfloat16)
            k_hi[t, j : j + sub, :] = top
            k_lo[t, j : j + sub, :] = (value - top.astype(jnp.float32)).astype(jnp.bfloat16)

    def multiply(t, dirs, accum):
        accum = accum + jnp.dot(dirs, k_hi[t], preferred_element_type=jnp.float32)
        return accum + jnp.dot(dirs, k_lo[t], preferred_element_type=jnp.float32)

    def first_of(t):
        return sixteen(slots_v[t, :, 0:n], slots_v[t, :, n:])

    def step(k, accum):
        arrive(slots_a, recv_a, at(k), msg)
        arrive(slots_v, recv_v, at(k - 1), msg_v)
        accum = multiply(at(k - 1), halves(first_of(at(k - 1))), accum)
        build(at(k))
        return accum

    zero = jnp.zeros((32, n), jnp.float32)
    arrive(slots_a, recv_a, at(0), msg)
    build(at(0))
    accum = lax.fori_loop(1, G, step, zero)
    arrive(slots_v, recv_v, at(G - 1), msg_v)
    accum = multiply(at(G - 1), halves(first_of(at(G - 1))), accum)

    def across(phase, accum):
        parts[phase, me_c] = accum[0:16] + accum[16:32]
        for k in range(1, C):
            copy_p(phase, k).start()
        for k in range(1, C):
            c = lax.rem(me_c + k, C)
            pltpu.make_async_remote_copy(
                src_ref=parts.at[phase, me_c], dst_ref=parts.at[phase, c], send_sem=send_p.at[phase, 0],
                recv_sem=recv_p.at[phase, c], device_id=(me_r, me_c), device_id_type=MESH).wait_recv()
        total = parts[phase, 0]
        for c in range(1, C):
            total = total + parts[phase, c]
        return total

    noise_row = noise[...]
    start = sixteen(signs, msg_v[:, n:])
    image = across(0, accum) + noise_row * start

    def dot(a, b):
        return jnp.sum(a * b, axis=1, keepdims=True)

    own_scal = scalars([dot(start, image), dot(image, image), dot(start, start)])
    vec[:, 0:n] = image[0:8]
    vec[:, n:] = jnp.zeros((8, LANES), jnp.float32)
    for k in range(n // LANES):
        vec[k : k + 1, n:] = image[8:9, k * LANES : (k + 1) * LANES]
    vec[7:8, n:] = own_scal
    scal_b[me_r] = own_scal

    def send_image(k):
        copy_b(k).start()
        for g in range(1, C):
            copy_s(k, g).start()

    over_targets(send_image)

    @pl.when(in_group)
    def _():
        slots_b[spot] = vec[...]

    def receive_image(b, carry):
        @pl.when(b != me_r)
        def _():
            @pl.when(b // G == me_c)
            def _():
                t = lax.rem(b, G)
                wait_slot(slots_b, recv_b, t, vec)
                scal_b[b] = slots_b[t, 7:8, n:]

            @pl.when(b // G != me_c)
            def _():
                wait_slot(scal_b, recv_s, b, own_c)
        return carry

    lax.fori_loop(0, R, receive_image, 0)
    total = jnp.sum(scal_b[...], axis=0)

    curve, square, norm = pick(total, 0), pick(total, 1), pick(total, 2)
    real = lax.broadcasted_iota(jnp.int32, (16, 1), 0) < 9
    alpha = jnp.where(real, norm / curve, 0.0)
    norm_next = alpha * alpha * square - norm
    beta = jnp.where(real, norm_next / norm, 0.0)

    def again(t, accum):
        first = first_of(t)
        moved = sixteen(slots_b[t, :, 0:n], slots_b[t, :, n:])
        return multiply(t, halves((first - alpha * moved) + beta * first), accum)

    accum = lax.fori_loop(0, G, again, zero, unroll=8)
    residual = start - alpha * image
    direction = residual + beta * start
    image = across(1, accum) + noise_row * direction
    own_scal = scalars([dot(direction, image)])
    own_c[...] = own_scal
    scal_c[me_r] = own_scal

    def send_curve(k):
        for g in range(C):
            copy_c(k, g).start()

    over_targets(send_curve)

    def receive_curve(b, carry):
        @pl.when(b != me_r)
        def _():
            wait_slot(scal_c, recv_c, b, own_c)
        return carry

    lax.fori_loop(0, R, receive_curve, 0)
    alpha_last = norm_next / pick(jnp.sum(scal_c[...], axis=0), 0)
    answer = alpha * start + alpha_last * direction
    residual = residual - alpha_last * image
    both[0] = answer
    both[1] = residual

    def finish(k):
        copy_a(k).wait_send()
        copy_v(k).wait_send()
        copy_b(k).wait_send()
        for g in range(1, C):
            copy_s(k, g).wait_send()
        for g in range(C):
            copy_c(k, g).wait_send()

    over_targets(finish)
    for phase in range(2):
        for k in range(1, C):
            copy_p(phase, k).wait_send()


def per_device(R, C, points, lengthscale, noise, target, probe_bits):
    n = points.shape[1]
    G = T = R // C
    f32, bf16, dma = jnp.float32, jnp.bfloat16, pltpu.SemaphoreType.DMA
    vmem = pl.BlockSpec(memory_space=pltpu.VMEM)
    both = pl.pallas_call(
        functools.partial(kernel, R, C),
        out_shape=jax.ShapeDtypeStruct((2, 16, n), f32),
        in_specs=[pl.BlockSpec(memory_space=pl.ANY)] * 5,
        out_specs=vmem,
        scratch_shapes=[
            pltpu.SMEM((8,), f32),
            pltpu.VMEM((8, n), f32),
            pltpu.VMEM((1, n), f32),
            pltpu.VMEM((1, n), f32),
            pltpu.VMEM((8, n), jnp.int32),
            pltpu.VMEM((8, n), f32),
            pltpu.VMEM((G, 8, n), f32),
            pltpu.VMEM((8, n + LANES), f32),
            pltpu.VMEM((G, 8, n + LANES), f32),
            pltpu.VMEM((2, C, 16, n), f32),
            pltpu.VMEM((8, n + LANES), f32),
            pltpu.VMEM((G, 8, n + LANES), f32),
            pltpu.VMEM((R, 1, LANES), f32),
            pltpu.VMEM((1, LANES), f32),
            pltpu.VMEM((R, 1, LANES), f32),
            pltpu.VMEM((G, n, n), bf16),
            pltpu.VMEM((G, n, n), bf16),
            dma((5,)), dma((T,)), dma((G,)), dma((T,)), dma((G,)), dma((2, C - 1)), dma((2, C)), dma((T,)), dma((G,)),
            dma((C - 1, T)), dma((R,)), dma((C, T)), dma((R,)),
        ],
        compiler_params=pltpu.CompilerParams(
            collective_id=0, has_side_effects=True, vmem_limit_bytes=60 * 1024 * 1024
        ),
    )(lengthscale, points, noise.reshape(1, n), target.reshape(1, n), probe_bits)
    return both[0, :9], both[1, :9]


def solution(mesh):
    return jax.shard_map(
        functools.partial(per_device, mesh.shape["row"], mesh.shape["col"]),
        mesh=mesh,
        in_specs=(P(None, "row"), P(), P("row"), P("row"), P(None, "row")),
        out_specs=(P(None, "row"), P(None, "row")),
        check_vma=False,
    )
```

```python
import functools

import jax
import jax.numpy as jnp
from jax import lax
from jax.experimental import pallas as pl
from jax.experimental.pallas import tpu as pltpu
from jax.sharding import PartitionSpec as P

MESH = pl.DeviceIdType.MESH
LANES = 128
root_five = 5.0**0.5


def split(x):
    high = x.astype(jnp.bfloat16).astype(jnp.float32)
    rest = x - high
    mid = rest.astype(jnp.bfloat16).astype(jnp.float32)
    return high, mid, rest - mid


def augment(points, own):
    high, mid, low = split(points)
    norms = split(jnp.sum(points * points, axis=0, keepdims=True))
    rows = lax.broadcasted_iota(jnp.int32, points.shape, 0)
    first = 3 if own else 0
    ends = jnp.where(rows < 6, 1.0, 0.0)
    for place in range(3):
        ends = jnp.where(rows == first + place, norms[place], ends)
    if own:
        high, mid, low = -2.0 * high, -2.0 * mid, -2.0 * low
        parts = [high, mid, high, low, high, mid]
    else:
        parts = [high, high, mid, high, low, mid]
    return jnp.concatenate(parts + [ends, jnp.zeros_like(ends)], axis=0)


def sixteen(probes, tile):
    n = probes.shape[1]
    line = jnp.concatenate([tile[k : k + 1, :] for k in range(n // LANES)], axis=1)
    rows = lax.broadcasted_iota(jnp.int32, probes.shape, 0)
    return jnp.concatenate([probes, jnp.where(rows == 0, line, 0.0)], axis=0)


def halves(x):
    high = x.astype(jnp.bfloat16)
    mid = (x - high.astype(jnp.float32)).astype(jnp.bfloat16)
    return jnp.concatenate([high, mid], axis=0)


def scalars(values):
    lanes = lax.broadcasted_iota(jnp.int32, (16, LANES), 1)
    rows = lax.broadcasted_iota(jnp.int32, (16, LANES), 0)
    spread = jnp.zeros((16, LANES), jnp.float32)
    for k, value in enumerate(values):
        spread = jnp.where(lanes == rows + 16 * k, value, spread)
    return jnp.sum(spread, axis=0, keepdims=True)


def pick(line, k):
    lanes = lax.broadcasted_iota(jnp.int32, (16, LANES), 1)
    rows = lax.broadcasted_iota(jnp.int32, (16, LANES), 0)
    return jnp.sum(jnp.where(lanes == rows + 16 * k, line, 0.0), axis=1, keepdims=True)


def kernel(R, C, scale_in, points_in, noise_in, target_in, bits_in, both,
           scale, points, noise, target, bits, msg, slots_a, msg_v, slots_v, parts, vec, slots_b, scal_b, own_c, scal_c, k_hi, k_lo,
           load, send_a, recv_a, send_v, recv_v, send_p, recv_p, send_b, recv_b, send_s, recv_s, send_c, recv_c):
    n = points.shape[1]
    G = R // C
    T = R // C
    sub = min(256, n)
    me_r = lax.axis_index("row")
    me_c = lax.axis_index("col")
    group = me_r // G
    spot = lax.rem(me_r, G)
    side = lax.rem(me_r, C)
    in_group = group == me_c

    loads = [
        pltpu.make_async_copy(source, here, load.at[k])
        for k, (source, here) in enumerate(
            [(scale_in, scale), (points_in, points), (bits_in, bits), (target_in, target), (noise_in, noise)])
    ]
    for one in loads:
        one.start()

    barrier = pltpu.get_barrier_semaphore()

    def greet(k, carry):
        pl.semaphore_signal(barrier, inc=1, device_id=(lax.rem(me_r + k, R), side), device_id_type=MESH)
        return carry

    lax.fori_loop(1, R, greet, 0)
    for k in range(1, C):
        pl.semaphore_signal(barrier, inc=1, device_id=(me_r, lax.rem(me_c + k, C)), device_id_type=MESH)

    for one in loads:
        one.wait()

    rows8 = lax.broadcasted_iota(jnp.int32, (8, 1), 0)
    lengths = jnp.full((8, 1), scale[0], jnp.float32)
    for f in range(1, 8):
        lengths = jnp.where(rows8 == f, scale[f], lengths)
    own_points = points[...] * (root_five / lengths)
    signs = 2.0 * bits[...].astype(jnp.float32) - 1.0
    own_target = target[...]
    msg[...] = own_points
    msg_v[:, 0:n] = signs
    msg_v[:, n:] = jnp.zeros((8, LANES), jnp.float32)
    for k in range(n // LANES):
        msg_v[k : k + 1, n:] = own_target[:, k * LANES : (k + 1) * LANES]

    pl.semaphore_wait(barrier, (T - jnp.where(side == me_c, 1, 0)) * C + C - 1)

    def target_row(k):
        return C * lax.rem(me_r // C + k, T) + me_c

    def copy_a(k):
        return pltpu.make_async_remote_copy(
            src_ref=msg, dst_ref=slots_a.at[spot], send_sem=send_a.at[k], recv_sem=recv_a.at[spot],
            device_id=(target_row(k), group), device_id_type=MESH)

    def copy_v(k):
        return pltpu.make_async_remote_copy(
            src_ref=msg_v, dst_ref=slots_v.at[spot], send_sem=send_v.at[k], recv_sem=recv_v.at[spot],
            device_id=(target_row(k), group), device_id_type=MESH)

    def copy_p(phase, k):
        return pltpu.make_async_remote_copy(
            src_ref=parts.at[phase, me_c], dst_ref=parts.at[phase, me_c],
            send_sem=send_p.at[phase, k - 1], recv_sem=recv_p.at[phase, me_c],
            device_id=(me_r, lax.rem(me_c + k, C)), device_id_type=MESH)

    def copy_b(k):
        return pltpu.make_async_remote_copy(
            src_ref=vec, dst_ref=slots_b.at[spot], send_sem=send_b.at[k], recv_sem=recv_b.at[spot],
            device_id=(target_row(k), group), device_id_type=MESH)

    def copy_s(k, g):
        return pltpu.make_async_remote_copy(
            src_ref=scal_b.at[me_r], dst_ref=scal_b.at[me_r], send_sem=send_s.at[g - 1, k], recv_sem=recv_s.at[me_r],
            device_id=(target_row(k), lax.rem(group + g, C)), device_id_type=MESH)

    def copy_c(k, g):
        return pltpu.make_async_remote_copy(
            src_ref=own_c, dst_ref=scal_c.at[me_r], send_sem=send_c.at[g, k], recv_sem=recv_c.at[me_r],
            device_id=(target_row(k), g), device_id_type=MESH)

    def over_targets(action):
        def one(k, carry):
            @pl.when(target_row(k) != me_r)
            def _():
                action(k)
            return carry
        lax.fori_loop(0, T, one, 0)

    over_targets(lambda k: copy_a(k).start())
    over_targets(lambda k: copy_v(k).start())

    @pl.when(in_group)
    def _():
        slots_a[spot] = msg[...]
        slots_v[spot] = msg_v[...]

    own_aug = augment(own_points, True).astype(jnp.bfloat16)

    def wait_slot(buffer, sem, t, like):
        pltpu.make_async_remote_copy(
            src_ref=like, dst_ref=buffer.at[t], send_sem=send_a.at[0], recv_sem=sem.at[t],
            device_id=(me_r, me_c), device_id_type=MESH).wait_recv()

    first_spot = jnp.where(in_group, spot, G - 1)

    def at(k):
        return lax.rem(first_spot - k + G, G)

    def arrive(buffer, sem, t, like):
        @pl.when(me_c * G + t != me_r)
        def _():
            wait_slot(buffer, sem, t, like)

    def build(t):
        columns = augment(slots_a[t], False).T.astype(jnp.bfloat16)
        for j in range(0, n, sub):
            s2 = jnp.dot(columns[j : j + sub, :], own_aug, preferred_element_type=jnp.float32)
            s2 = jnp.maximum(s2, 1e-12)
            s = s2 * lax.rsqrt(s2)
            value = (s2 * (1.0 / 3.0) + s + 1.0) * jnp.exp(-s)
            top = value.astype(jnp.bfloat16)
            k_hi[t, j : j + sub, :] = top
            k_lo[t, j : j + sub, :] = (value - top.astype(jnp.float32)).astype(jnp.bfloat16)

    def multiply(t, dirs, accum):
        accum = accum + jnp.dot(dirs, k_hi[t], preferred_element_type=jnp.float32)
        return accum + jnp.dot(dirs, k_lo[t], preferred_element_type=jnp.float32)

    def first_of(t):
        return sixteen(slots_v[t, :, 0:n], slots_v[t, :, n:])

    def construct(k, carry):
        arrive(slots_a, recv_a, at(k), msg)
        build(at(k))
        return carry

    def gather(k, carry):
        arrive(slots_v, recv_v, at(k), msg_v)
        return carry

    def product(t, accum):
        return multiply(t, halves(first_of(t)), accum)

    zero = jnp.zeros((32, n), jnp.float32)
    lax.fori_loop(0, G, construct, 0)
    lax.fori_loop(0, G, gather, 0)
    accum = lax.fori_loop(0, G, product, zero, unroll=8)

    def across(phase, accum):
        parts[phase, me_c] = accum[0:16] + accum[16:32]
        for k in range(1, C):
            copy_p(phase, k).start()
        for k in range(1, C):
            c = lax.rem(me_c + k, C)
            pltpu.make_async_remote_copy(
                src_ref=parts.at[phase, me_c], dst_ref=parts.at[phase, c], send_sem=send_p.at[phase, 0],
                recv_sem=recv_p.at[phase, c], device_id=(me_r, me_c), device_id_type=MESH).wait_recv()
        total = parts[phase, 0]
        for c in range(1, C):
            total = total + parts[phase, c]
        return total

    noise_row = noise[...]
    start = sixteen(signs, msg_v[:, n:])
    image = across(0, accum) + noise_row * start

    def dot(a, b):
        return jnp.sum(a * b, axis=1, keepdims=True)

    own_scal = scalars([dot(start, image), dot(image, image), dot(start, start)])
    vec[:, 0:n] = image[0:8]
    vec[:, n:] = jnp.zeros((8, LANES), jnp.float32)
    for k in range(n // LANES):
        vec[k : k + 1, n:] = image[8:9, k * LANES : (k + 1) * LANES]
    vec[7:8, n:] = own_scal
    scal_b[me_r] = own_scal

    def send_image(k):
        copy_b(k).start()
        for g in range(1, C):
            copy_s(k, g).start()

    over_targets(send_image)

    @pl.when(in_group)
    def _():
        slots_b[spot] = vec[...]

    def receive_image(b, carry):
        @pl.when(b != me_r)
        def _():
            @pl.when(b // G == me_c)
            def _():
                t = lax.rem(b, G)
                wait_slot(slots_b, recv_b, t, vec)
                scal_b[b] = slots_b[t, 7:8, n:]

            @pl.when(b // G != me_c)
            def _():
                wait_slot(scal_b, recv_s, b, own_c)
        return carry

    lax.fori_loop(0, R, receive_image, 0)
    total = jnp.sum(scal_b[...], axis=0)

    curve, square, norm = pick(total, 0), pick(total, 1), pick(total, 2)
    real = lax.broadcasted_iota(jnp.int32, (16, 1), 0) < 9
    alpha = jnp.where(real, norm / curve, 0.0)
    norm_next = alpha * alpha * square - norm
    beta = jnp.where(real, norm_next / norm, 0.0)

    def again(t, accum):
        first = first_of(t)
        moved = sixteen(slots_b[t, :, 0:n], slots_b[t, :, n:])
        return multiply(t, halves((first - alpha * moved) + beta * first), accum)

    accum = lax.fori_loop(0, G, again, zero, unroll=8)
    residual = start - alpha * image
    direction = residual + beta * start
    image = across(1, accum) + noise_row * direction
    own_scal = scalars([dot(direction, image)])
    own_c[...] = own_scal
    scal_c[me_r] = own_scal

    def send_curve(k):
        for g in range(C):
            copy_c(k, g).start()

    over_targets(send_curve)

    def receive_curve(b, carry):
        @pl.when(b != me_r)
        def _():
            wait_slot(scal_c, recv_c, b, own_c)
        return carry

    lax.fori_loop(0, R, receive_curve, 0)
    alpha_last = norm_next / pick(jnp.sum(scal_c[...], axis=0), 0)
    answer = alpha * start + alpha_last * direction
    residual = residual - alpha_last * image
    both[0] = answer
    both[1] = residual

    def finish(k):
        copy_a(k).wait_send()
        copy_v(k).wait_send()
        copy_b(k).wait_send()
        for g in range(1, C):
            copy_s(k, g).wait_send()
        for g in range(C):
            copy_c(k, g).wait_send()

    over_targets(finish)
    for phase in range(2):
        for k in range(1, C):
            copy_p(phase, k).wait_send()


def per_device(R, C, points, lengthscale, noise, target, probe_bits):
    n = points.shape[1]
    G = T = R // C
    f32, bf16, dma = jnp.float32, jnp.bfloat16, pltpu.SemaphoreType.DMA
    vmem = pl.BlockSpec(memory_space=pltpu.VMEM)
    both = pl.pallas_call(
        functools.partial(kernel, R, C),
        out_shape=jax.ShapeDtypeStruct((2, 16, n), f32),
        in_specs=[pl.BlockSpec(memory_space=pl.ANY)] * 5,
        out_specs=vmem,
        scratch_shapes=[
            pltpu.SMEM((8,), f32),
            pltpu.VMEM((8, n), f32),
            pltpu.VMEM((1, n), f32),
            pltpu.VMEM((1, n), f32),
            pltpu.VMEM((8, n), jnp.int32),
            pltpu.VMEM((8, n), f32),
            pltpu.VMEM((G, 8, n), f32),
            pltpu.VMEM((8, n + LANES), f32),
            pltpu.VMEM((G, 8, n + LANES), f32),
            pltpu.VMEM((2, C, 16, n), f32),
            pltpu.VMEM((8, n + LANES), f32),
            pltpu.VMEM((G, 8, n + LANES), f32),
            pltpu.VMEM((R, 1, LANES), f32),
            pltpu.VMEM((1, LANES), f32),
            pltpu.VMEM((R, 1, LANES), f32),
            pltpu.VMEM((G, n, n), bf16),
            pltpu.VMEM((G, n, n), bf16),
            dma((5,)), dma((T,)), dma((G,)), dma((T,)), dma((G,)), dma((2, C - 1)), dma((2, C)), dma((T,)), dma((G,)),
            dma((C - 1, T)), dma((R,)), dma((C, T)), dma((R,)),
        ],
        compiler_params=pltpu.CompilerParams(
            collective_id=0, has_side_effects=True, vmem_limit_bytes=60 * 1024 * 1024
        ),
    )(lengthscale, points, noise.reshape(1, n), target.reshape(1, n), probe_bits)
    return both[0, :9], both[1, :9]


def solution(mesh):
    return jax.shard_map(
        functools.partial(per_device, mesh.shape["row"], mesh.shape["col"]),
        mesh=mesh,
        in_specs=(P(None, "row"), P(), P("row"), P("row"), P(None, "row")),
        out_specs=(P(None, "row"), P(None, "row")),
        check_vma=False,
    )
```

```python
import functools

import jax
import jax.numpy as jnp
from jax import lax
from jax.experimental import pallas as pl
from jax.experimental.pallas import tpu as pltpu
from jax.sharding import PartitionSpec as P

MESH = pl.DeviceIdType.MESH
LANES = 128
root_five = 5.0**0.5


def split(x):
    high = x.astype(jnp.bfloat16).astype(jnp.float32)
    rest = x - high
    mid = rest.astype(jnp.bfloat16).astype(jnp.float32)
    return high, mid, rest - mid


def augment(points, own):
    high, mid, low = split(points)
    norms = split(jnp.sum(points * points, axis=0, keepdims=True))
    rows = lax.broadcasted_iota(jnp.int32, points.shape, 0)
    first = 3 if own else 0
    ends = jnp.where(rows < 6, 1.0, 0.0)
    for place in range(3):
        ends = jnp.where(rows == first + place, norms[place], ends)
    if own:
        high, mid, low = -2.0 * high, -2.0 * mid, -2.0 * low
        parts = [high, mid, high, low, high, mid]
    else:
        parts = [high, high, mid, high, low, mid]
    return jnp.concatenate(parts + [ends, jnp.zeros_like(ends)], axis=0)


def sixteen(probes, tile):
    n = probes.shape[1]
    line = jnp.concatenate([tile[k : k + 1, :] for k in range(n // LANES)], axis=1)
    rows = lax.broadcasted_iota(jnp.int32, probes.shape, 0)
    return jnp.concatenate([probes, jnp.where(rows == 0, line, 0.0)], axis=0)


def halves(x):
    high = x.astype(jnp.bfloat16)
    mid = (x - high.astype(jnp.float32)).astype(jnp.bfloat16)
    return jnp.concatenate([high, mid], axis=0)


def scalars(values):
    lanes = lax.broadcasted_iota(jnp.int32, (16, LANES), 1)
    rows = lax.broadcasted_iota(jnp.int32, (16, LANES), 0)
    spread = jnp.zeros((16, LANES), jnp.float32)
    for k, value in enumerate(values):
        spread = jnp.where(lanes == rows + 16 * k, value, spread)
    return jnp.sum(spread, axis=0, keepdims=True)


def pick(line, k):
    lanes = lax.broadcasted_iota(jnp.int32, (16, LANES), 1)
    rows = lax.broadcasted_iota(jnp.int32, (16, LANES), 0)
    return jnp.sum(jnp.where(lanes == rows + 16 * k, line, 0.0), axis=1, keepdims=True)


def kernel(R, C, scale_in, points_in, noise_in, target_in, bits_in, both,
           scale, points, noise, target, bits, msg, slots_a, msg_v, slots_v, parts, vec, slots_b, scal_b, own_c, scal_c, k_hi, k_lo,
           load, send_a, recv_a, send_v, recv_v, send_p, recv_p, send_b, recv_b, send_s, recv_s, send_c, recv_c):
    n = points.shape[1]
    G = R // C
    T = R // C
    sub = min(256, n)
    me_r = lax.axis_index("row")
    me_c = lax.axis_index("col")
    group = me_r // G
    spot = lax.rem(me_r, G)
    side = lax.rem(me_r, C)
    in_group = group == me_c

    loads = [
        pltpu.make_async_copy(source, here, load.at[k])
        for k, (source, here) in enumerate(
            [(scale_in, scale), (points_in, points), (bits_in, bits), (target_in, target), (noise_in, noise)])
    ]
    for one in loads:
        one.start()

    barrier = pltpu.get_barrier_semaphore()

    def greet(k, carry):
        pl.semaphore_signal(barrier, inc=1, device_id=(lax.rem(me_r + k, R), side), device_id_type=MESH)
        return carry

    lax.fori_loop(1, R, greet, 0)
    for k in range(1, C):
        pl.semaphore_signal(barrier, inc=1, device_id=(me_r, lax.rem(me_c + k, C)), device_id_type=MESH)

    for one in loads:
        one.wait()

    rows8 = lax.broadcasted_iota(jnp.int32, (8, 1), 0)
    lengths = jnp.full((8, 1), scale[0], jnp.float32)
    for f in range(1, 8):
        lengths = jnp.where(rows8 == f, scale[f], lengths)
    own_points = points[...] * (root_five / lengths)
    signs = 2.0 * bits[...].astype(jnp.float32) - 1.0
    own_target = target[...]
    msg[...] = own_points
    msg_v[:, 0:n] = signs
    msg_v[:, n:] = jnp.zeros((8, LANES), jnp.float32)
    for k in range(n // LANES):
        msg_v[k : k + 1, n:] = own_target[:, k * LANES : (k + 1) * LANES]

    pl.semaphore_wait(barrier, (T - jnp.where(side == me_c, 1, 0)) * C + C - 1)

    def target_row(k):
        return C * lax.rem(me_r // C + k, T) + me_c

    def copy_a(k):
        return pltpu.make_async_remote_copy(
            src_ref=msg, dst_ref=slots_a.at[spot], send_sem=send_a.at[k], recv_sem=recv_a.at[spot],
            device_id=(target_row(k), group), device_id_type=MESH)

    def copy_v(k):
        return pltpu.make_async_remote_copy(
            src_ref=msg_v, dst_ref=slots_v.at[spot], send_sem=send_v.at[k], recv_sem=recv_v.at[spot],
            device_id=(target_row(k), group), device_id_type=MESH)

    def copy_p(phase, k):
        return pltpu.make_async_remote_copy(
            src_ref=parts.at[phase, me_c], dst_ref=parts.at[phase, me_c],
            send_sem=send_p.at[phase, k - 1], recv_sem=recv_p.at[phase, me_c],
            device_id=(me_r, lax.rem(me_c + k, C)), device_id_type=MESH)

    def copy_b(k):
        return pltpu.make_async_remote_copy(
            src_ref=vec, dst_ref=slots_b.at[spot], send_sem=send_b.at[k], recv_sem=recv_b.at[spot],
            device_id=(target_row(k), group), device_id_type=MESH)

    def copy_s(k, g):
        return pltpu.make_async_remote_copy(
            src_ref=scal_b.at[me_r], dst_ref=scal_b.at[me_r], send_sem=send_s.at[g - 1, k], recv_sem=recv_s.at[me_r],
            device_id=(target_row(k), lax.rem(group + g, C)), device_id_type=MESH)

    def copy_c(k, g):
        return pltpu.make_async_remote_copy(
            src_ref=own_c, dst_ref=scal_c.at[me_r], send_sem=send_c.at[g, k], recv_sem=recv_c.at[me_r],
            device_id=(target_row(k), g), device_id_type=MESH)

    def over_targets(action):
        def one(k, carry):
            @pl.when(target_row(k) != me_r)
            def _():
                action(k)
            return carry
        lax.fori_loop(0, T, one, 0)

    over_targets(lambda k: copy_a(k).start())
    over_targets(lambda k: copy_v(k).start())

    @pl.when(in_group)
    def _():
        slots_a[spot] = msg[...]
        slots_v[spot] = msg_v[...]

    own_aug = augment(own_points, True).astype(jnp.bfloat16)

    def wait_slot(buffer, sem, t, like):
        pltpu.make_async_remote_copy(
            src_ref=like, dst_ref=buffer.at[t], send_sem=send_a.at[0], recv_sem=sem.at[t],
            device_id=(me_r, me_c), device_id_type=MESH).wait_recv()

    first_spot = jnp.where(in_group, spot, G - 1)

    def at(k):
        return lax.rem(first_spot - k + G, G)

    def arrive(buffer, sem, t, like):
        @pl.when(me_c * G + t != me_r)
        def _():
            wait_slot(buffer, sem, t, like)

    def build(t):
        columns = augment(slots_a[t], False).T.astype(jnp.bfloat16)
        for j in range(0, n, sub):
            s2 = jnp.dot(columns[j : j + sub, :], own_aug, preferred_element_type=jnp.float32)
            s2 = jnp.maximum(s2, 1e-12)
            s = s2 * lax.rsqrt(s2)
            value = (s2 * (1.0 / 3.0) + s + 1.0) * jnp.exp(-s)
            top = value.astype(jnp.bfloat16)
            k_hi[t, j : j + sub, :] = top
            k_lo[t, j : j + sub, :] = (value - top.astype(jnp.float32)).astype(jnp.bfloat16)

    def multiply(t, dirs, accum):
        accum = accum + jnp.dot(dirs, k_hi[t], preferred_element_type=jnp.float32)
        return accum + jnp.dot(dirs, k_lo[t], preferred_element_type=jnp.float32)

    def first_of(t):
        return sixteen(slots_v[t, :, 0:n], slots_v[t, :, n:])

    def construct(k, carry):
        arrive(slots_a, recv_a, at(k), msg)
        build(at(k))
        return carry

    def gather(k, carry):
        arrive(slots_v, recv_v, at(k), msg_v)
        return carry

    def product(t, accum):
        return multiply(t, halves(first_of(t)), accum)

    zero = jnp.zeros((32, n), jnp.float32)
    lax.fori_loop(0, G, construct, 0)
    lax.fori_loop(0, G, gather, 0)
    accum = lax.fori_loop(0, G, product, zero, unroll=8)

    def across(phase, accum):
        parts[phase, me_c] = accum[0:16] + accum[16:32]
        for k in range(1, C):
            copy_p(phase, k).start()
        for k in range(1, C):
            c = lax.rem(me_c + k, C)
            pltpu.make_async_remote_copy(
                src_ref=parts.at[phase, me_c], dst_ref=parts.at[phase, c], send_sem=send_p.at[phase, 0],
                recv_sem=recv_p.at[phase, c], device_id=(me_r, me_c), device_id_type=MESH).wait_recv()
        total = parts[phase, 0]
        for c in range(1, C):
            total = total + parts[phase, c]
        return total

    noise_row = noise[...]
    start = sixteen(signs, msg_v[:, n:])
    image = across(0, accum) + noise_row * start

    def dot(a, b):
        return jnp.sum(a * b, axis=1, keepdims=True)

    own_scal = scalars([dot(start, image), dot(image, image), dot(start, start)])
    vec[:, 0:n] = image[0:8]
    vec[:, n:] = jnp.zeros((8, LANES), jnp.float32)
    for k in range(n // LANES):
        vec[k : k + 1, n:] = image[8:9, k * LANES : (k + 1) * LANES]
    vec[7:8, n:] = own_scal
    scal_b[me_r] = own_scal

    def send_image(k):
        copy_b(k).start()

    def send_dots(k):
        for g in range(1, C):
            copy_s(k, g).start()

    over_targets(send_dots)
    over_targets(send_image)

    @pl.when(in_group)
    def _():
        slots_b[spot] = vec[...]

    def receive_image(b, carry):
        @pl.when(b != me_r)
        def _():
            @pl.when(b // G == me_c)
            def _():
                t = lax.rem(b, G)
                wait_slot(slots_b, recv_b, t, vec)
                scal_b[b] = slots_b[t, 7:8, n:]

            @pl.when(b // G != me_c)
            def _():
                wait_slot(scal_b, recv_s, b, own_c)
        return carry

    lax.fori_loop(0, R, receive_image, 0)
    total = jnp.sum(scal_b[...], axis=0)

    curve, square, norm = pick(total, 0), pick(total, 1), pick(total, 2)
    real = lax.broadcasted_iota(jnp.int32, (16, 1), 0) < 9
    alpha = jnp.where(real, norm / curve, 0.0)
    norm_next = alpha * alpha * square - norm
    beta = jnp.where(real, norm_next / norm, 0.0)

    def again(t, accum):
        first = first_of(t)
        moved = sixteen(slots_b[t, :, 0:n], slots_b[t, :, n:])
        return multiply(t, halves((first - alpha * moved) + beta * first), accum)

    accum = lax.fori_loop(0, G, again, zero, unroll=8)
    residual = start - alpha * image
    direction = residual + beta * start
    image = across(1, accum) + noise_row * direction
    own_scal = scalars([dot(direction, image)])
    own_c[...] = own_scal
    scal_c[me_r] = own_scal

    def send_curve(k):
        for g in range(C):
            copy_c(k, g).start()

    over_targets(send_curve)

    def receive_curve(b, carry):
        @pl.when(b != me_r)
        def _():
            wait_slot(scal_c, recv_c, b, own_c)
        return carry

    lax.fori_loop(0, R, receive_curve, 0)
    alpha_last = norm_next / pick(jnp.sum(scal_c[...], axis=0), 0)
    answer = alpha * start + alpha_last * direction
    residual = residual - alpha_last * image
    both[0] = answer
    both[1] = residual

    def finish(k):
        copy_a(k).wait_send()
        copy_v(k).wait_send()
        copy_b(k).wait_send()
        for g in range(1, C):
            copy_s(k, g).wait_send()
        for g in range(C):
            copy_c(k, g).wait_send()

    over_targets(finish)
    for phase in range(2):
        for k in range(1, C):
            copy_p(phase, k).wait_send()


def per_device(R, C, points, lengthscale, noise, target, probe_bits):
    n = points.shape[1]
    G = T = R // C
    f32, bf16, dma = jnp.float32, jnp.bfloat16, pltpu.SemaphoreType.DMA
    vmem = pl.BlockSpec(memory_space=pltpu.VMEM)
    both = pl.pallas_call(
        functools.partial(kernel, R, C),
        out_shape=jax.ShapeDtypeStruct((2, 16, n), f32),
        in_specs=[pl.BlockSpec(memory_space=pl.ANY)] * 5,
        out_specs=vmem,
        scratch_shapes=[
            pltpu.SMEM((8,), f32),
            pltpu.VMEM((8, n), f32),
            pltpu.VMEM((1, n), f32),
            pltpu.VMEM((1, n), f32),
            pltpu.VMEM((8, n), jnp.int32),
            pltpu.VMEM((8, n), f32),
            pltpu.VMEM((G, 8, n), f32),
            pltpu.VMEM((8, n + LANES), f32),
            pltpu.VMEM((G, 8, n + LANES), f32),
            pltpu.VMEM((2, C, 16, n), f32),
            pltpu.VMEM((8, n + LANES), f32),
            pltpu.VMEM((G, 8, n + LANES), f32),
            pltpu.VMEM((R, 1, LANES), f32),
            pltpu.VMEM((1, LANES), f32),
            pltpu.VMEM((R, 1, LANES), f32),
            pltpu.VMEM((G, n, n), bf16),
            pltpu.VMEM((G, n, n), bf16),
            dma((5,)), dma((T,)), dma((G,)), dma((T,)), dma((G,)), dma((2, C - 1)), dma((2, C)), dma((T,)), dma((G,)),
            dma((C - 1, T)), dma((R,)), dma((C, T)), dma((R,)),
        ],
        compiler_params=pltpu.CompilerParams(
            collective_id=0, has_side_effects=True, vmem_limit_bytes=60 * 1024 * 1024
        ),
    )(lengthscale, points, noise.reshape(1, n), target.reshape(1, n), probe_bits)
    return both[0, :9], both[1, :9]


def solution(mesh):
    return jax.shard_map(
        functools.partial(per_device, mesh.shape["row"], mesh.shape["col"]),
        mesh=mesh,
        in_specs=(P(None, "row"), P(), P("row"), P("row"), P(None, "row")),
        out_specs=(P(None, "row"), P(None, "row")),
        check_vma=False,
    )
```
